512 devices in a mesh: dp: 16 (over y, core), attn: 32 (over x, z).
Axes of the slice: x: 4, y: 8, z: 8, core: 2. Of those that a mesh axis runs over, the one named last changes fastest.
Arguments:
- query_states: bfloat16 [65536, 4096], P(('dp', 'attn')), may hold values from -96 to 96
- key_states: bfloat16 [65536, 512], P(('dp', 'attn')), may hold values from -4.5 to 4.5
- value_states: bfloat16 [65536, 512], P(('dp', 'attn')), may hold values from -6 to 6
- out_grad: bfloat16 [65536, 4096], P(('dp', 'attn')), may hold values from -24 to 24
- doc_lengths: int32 [16, 12], P('dp'), may hold values from 1 to 384, 4096 in all within a row
- layer_inputs: bfloat16 [4096, 65536], P(None, ('dp', 'attn')), may hold values from -24 to 24
Outputs:
- query_grad: bfloat16 [65536, 4096], P(('dp', 'attn'))
- weight_grad: float32 [4096, 1024], P(('dp', 'attn'))
The draws below stay inside these ranges and needn't reach their ends.
Inputs may be any that keep to these rules, and one draw needn't show every extreme that they name: `doc_lengths`: row g lists the lengths of the documents of data group g in the order in which they lie in its pack; they sum to 4096, and the longest is exactly 384.
All inputs are finite; a program needn't handle non-finite values.
Results may differ from the reference program's by a relative error of at most 0.0051.
Values may be sent and summed in bfloat16 or wider, within the bound.
A program may use at most 64 MiB of HBM per device.

```python
import math
import jax
import jax.numpy as jnp
import numpy as np
from jax import lax

D = 4096
HQ = 32
KVH = 4
DH = 128
GROUP = 8
TOK_DEV = 128
NDOC = 12
MOST = 384
GROUP_TOK = 4096
TOKENS = 65536
N_DP = 16


def paired_draw(key):
    key_base = jax.random.fold_in(key, 11)
    query_base = jax.random.fold_in(key, 12)
    base_keys = jnp.clip(jax.random.normal(key_base, (TOKENS, KVH * DH), jnp.float32), -4.0, 4.0)
    base_queries = jnp.clip(jax.random.normal(query_base, (TOKENS, HQ * DH), jnp.float32), -4.0, 4.0)
    keys_out = base_keys
    queries_out = base_queries
    return (queries_out, keys_out)


def draw_query_states(key, part):
    queries_out, keys_out = paired_draw(key)
    return queries_out.astype(jnp.bfloat16)


def draw_key_states(key, part):
    queries_out, keys_out = paired_draw(key)
    return keys_out.astype(jnp.bfloat16)


def with_spikes(result, own_key, source, target, blocks, factor):
    owner, partner = [(jnp.arange(result.shape[dim]) // (result.shape[dim] // blocks)).reshape([-1 if axis == dim else 1 for axis in range(result.ndim)]) for dim in (source, target)]
    chosen = jax.random.permutation(own_key, blocks)[partner]
    strong = (owner == chosen) | (owner == (partner + blocks // 2) % blocks)
    return jnp.where(strong, factor * result, result)


def shard_levels(rng, dims, pieces, least, high):
    gain = 1.0
    for axis_at, blocks in pieces:
        draws = jax.random.uniform(jax.random.fold_in(jax.random.fold_in(rng, 6), axis_at), (blocks,), jnp.float32, least / len(pieces), high / len(pieces))
        gain = gain * jnp.repeat(jnp.exp(draws), dims[axis_at] // blocks).reshape((-1,) + (1,) * (len(dims) - 1 - axis_at))
    return gain


def length_profile(number_of, total, reach, lean):
    portions = [(1 << 20) // math.isqrt(rank ** lean) + 1 for rank in range(2, number_of + 1)]
    spare, holding = total - reach - (number_of - 1), [1] * (number_of - 1)
    while spare > 0:
        candidates = [i for i in range(number_of - 1) if holding[i] < reach]
        mass, remaining = sum([portions[i] for i in candidates]), spare
        for i in candidates:
            more = min(reach - holding[i], max(1, remaining * portions[i] // mass), spare)
            holding[i] = holding[i] + more
            spare = spare - more
    return np.array([reach] + holding)


def uneven_parts(key, number_of, total, limit, skew):
    if number_of == 2:
        one = jax.random.randint(key, (), max(1, total - limit), min(limit, total - 1) + 1)
        return jnp.stack([one, total - one])
    tallies = jnp.asarray(length_profile(number_of, total, limit, skew), jnp.int32)
    pairs = (number_of - 1) // 2
    donor, receiver = tallies[1:1 + 2 * pairs:2], tallies[2:2 + 2 * pairs:2]
    room = jnp.minimum(donor - 1, limit - receiver)
    shifted = jax.random.randint(jax.random.fold_in(key, 1), (pairs,), 0, 1 << 20) % (room + 1)
    tallies = tallies.at[1:1 + 2 * pairs:2].set(donor - shifted).at[2:2 + 2 * pairs:2].set(receiver + shifted)
    return tallies[jax.random.permutation(jax.random.fold_in(key, 2), number_of)]


def gaussian(key, dims, width, limit, pieces=(), kind=jnp.bfloat16):
    array = jax.random.normal(key, dims, jnp.float32) * width
    if len(pieces) > 0:
        array = shard_levels(key, dims, pieces, -0.22, 0.18) * array
    return jnp.clip(array, min=-limit, max=limit).astype(kind)


def bell_draw_with(stream_key, extent, deviation, reach, shards, heavy, kind=jnp.bfloat16):
    result = deviation * jax.random.normal(stream_key, extent, jnp.float32)
    if shards:
        result = result * shard_levels(stream_key, extent, shards, -0.22, 0.18)
    return jnp.clip(with_spikes(result, jax.random.fold_in(stream_key, 3), *heavy), -reach, reach).astype(kind)


def setup_inputs(seed: int = 0) -> dict:
    arg_keys = jax.random.split(jax.random.key(seed), 7)
    query_states = draw_query_states(jax.random.fold_in(arg_keys[6], 71), 0)
    key_states = draw_key_states(jax.random.fold_in(arg_keys[6], 71), 0)
    value_states = gaussian(arg_keys[2], (TOKENS, KVH * DH), 1.0, 6.0, ((0, 512),))
    out_grad = gaussian(arg_keys[3], (TOKENS, HQ * DH), 4.0, 24.0, ((0, 512),))
    doc_lengths = jax.vmap(lambda own: uneven_parts(own, NDOC, GROUP_TOK, MOST, 2))(jax.random.split(arg_keys[4], N_DP)).reshape((N_DP, NDOC)).astype(jnp.int32)
    layer_inputs = bell_draw_with(arg_keys[5], (D, TOKENS), 1.0, 24.0, ((1, 512),), (1, 0, 512, 6.0))
    return dict(query_states=query_states, key_states=key_states, value_states=value_states, out_grad=out_grad, doc_lengths=doc_lengths, layer_inputs=layer_inputs)


masked_score = -1e30


def doc_index(position, bounds):
    return jnp.sum((position[:, None] >= bounds[None, :]).astype(jnp.int32), axis=1).astype(jnp.int32)


def group_grads(group_queries, group_keys, group_values, group_out, lengths):
    bounds = jnp.cumsum(lengths).astype(jnp.int32)
    padding = jnp.zeros((MOST, KVH * DH), group_keys.dtype)
    key_padded = jnp.concatenate([padding, group_keys], axis=0)
    value_padded = jnp.concatenate([padding, group_values], axis=0)
    score_scale = DH ** -0.5
    window = TOK_DEV + MOST

    def one_block(running, block_index):
        first_row = (block_index * TOK_DEV).astype(jnp.int32)
        query_block = lax.dynamic_slice_in_dim(group_queries, first_row, TOK_DEV, 0).astype(jnp.float32).reshape(TOK_DEV, KVH, GROUP, DH)
        grad_block = lax.dynamic_slice_in_dim(group_out, first_row, TOK_DEV, 0).astype(jnp.float32).reshape(TOK_DEV, KVH, GROUP, DH)
        key_window = lax.dynamic_slice_in_dim(key_padded, first_row, window, 0).astype(jnp.float32).reshape(window, KVH, DH)
        value_window = lax.dynamic_slice_in_dim(value_padded, first_row, window, 0).astype(jnp.float32).reshape(window, KVH, DH)
        query_pos = first_row + jnp.arange(TOK_DEV, dtype=jnp.int32)
        key_pos = first_row - MOST + jnp.arange(window, dtype=jnp.int32)
        allowed = (key_pos[None, :] >= 0) & (key_pos[None, :] <= query_pos[:, None])
        allowed = allowed & (doc_index(query_pos, bounds)[:, None] == doc_index(key_pos, bounds)[None, :])
        scores = score_scale * jnp.einsum("tgjd,ugd->gjtu", query_block, key_window)
        scores = jnp.where(allowed, scores, masked_score)
        row_max = jnp.max(scores, axis=-1, keepdims=True)
        weights = jnp.exp(scores - row_max)
        probs = weights / jnp.sum(weights, axis=-1, keepdims=True)
        dprobs = jnp.einsum("tgjd,ugd->gjtu", grad_block, value_window)
        row_delta = jnp.sum(probs * dprobs, axis=-1, keepdims=True)
        dscores = lax.optimization_barrier((probs * (dprobs - row_delta)).astype(jnp.bfloat16)).astype(jnp.float32)
        probs_low = lax.optimization_barrier(probs.astype(jnp.bfloat16)).astype(jnp.float32)
        query_grad = (score_scale * jnp.einsum("gjtu,ugd->tgjd", dscores, key_window)).astype(jnp.bfloat16)
        key_grad = score_scale * jnp.einsum("gjtu,tgjd->ugd", dscores, query_block)
        value_grad = jnp.einsum("gjtu,tgjd->ugd", probs_low, grad_block)
        both = jnp.stack([key_grad, value_grad]).reshape(2, window, KVH * DH)
        current = lax.dynamic_slice_in_dim(running, first_row, window, 1)
        running = lax.dynamic_update_slice_in_dim(running, current + both, first_row, 1)
        return running, query_grad.reshape(TOK_DEV, HQ * DH)

    initial = jnp.zeros((2, GROUP_TOK + MOST, KVH * DH), jnp.float32)
    totals, query_grads = lax.scan(one_block, initial, jnp.arange(GROUP_TOK // TOK_DEV, dtype=jnp.int32))
    kv_rows = jnp.concatenate([totals[0, MOST:], totals[1, MOST:]], axis=1).astype(jnp.bfloat16)
    return query_grads.reshape(GROUP_TOK, HQ * DH), kv_rows


def reference(query_states, key_states, value_states, out_grad, doc_lengths, layer_inputs):
    def per_group(running, group_index):
        first_row = (group_index * GROUP_TOK).astype(jnp.int32)
        group_queries = lax.dynamic_slice_in_dim(query_states, first_row, GROUP_TOK, 0)
        group_keys = lax.dynamic_slice_in_dim(key_states, first_row, GROUP_TOK, 0)
        group_values = lax.dynamic_slice_in_dim(value_states, first_row, GROUP_TOK, 0)
        group_out = lax.dynamic_slice_in_dim(out_grad, first_row, GROUP_TOK, 0)
        lengths = lax.dynamic_index_in_dim(doc_lengths, group_index, 0, keepdims=False)
        query_grad, kv_rows = group_grads(group_queries, group_keys, group_values, group_out, lengths)
        group_inputs = lax.dynamic_slice_in_dim(layer_inputs, first_row, GROUP_TOK, 1)
        running = running + jnp.dot(group_inputs, kv_rows, preferred_element_type=jnp.float32)
        return running, query_grad

    initial = jnp.zeros((D, 2 * KVH * DH), jnp.float32)
    weight_total, query_grads = lax.scan(per_group, initial, jnp.arange(N_DP, dtype=jnp.int32))
    return query_grads.reshape(TOKENS, HQ * DH), weight_total * (float(TOKENS) ** -0.5)
```

```python
import functools

import jax
import jax.numpy as jnp
from jax import lax
from jax.experimental import pallas as pl
from jax.experimental.pallas import tpu as pltpu
from jax.sharding import PartitionSpec as P

DH = 128
SPAN = 3
NX, NY, NZ = 4, 8, 8
MEMBERS = 8
HEADS = 4
TOK = 128
LOG2E = 1.4426950408889634
HIDDEN = -1e30

IN0, IN1, IN2, ATT, OUT2, OUT3, OUT4, MUL, SUMY, SUMZ = range(10)
STEPS = HEADS + SUMZ


def kernel(
    doc_ref, q_ref, k_ref, v_ref, og_ref, x_ref, dq_ref, w_ref,
    kv, bias, probs, dscores, parts, osend, orecv, rows, xin, wsend, yrecv, zsend, zrecv,
    in_s, in_r, out_s, out_r, x_s, x_r, x_own, ag_s, ag_r, y_s, y_r, z_s, z_r,
):
    f32, bf16 = jnp.float32, jnp.bfloat16
    attn, dp = lax.axis_index("attn"), lax.axis_index("dp")
    x, z = attn // NZ, lax.rem(attn, NZ)
    y, core = dp // 2, lax.rem(dp, 2)
    right = (dp, lax.rem(attn + 1, NX * NZ))
    left = (dp, lax.rem(attn + NX * NZ - 1, NX * NZ))

    def in_team(r):
        c = lax.rem(core + r // NX, 2)
        return (y * 2 + c, lax.rem(x + lax.rem(r, NX), NX) * NZ + z)

    def in_y(s):
        return (lax.rem(y + s, NY) * 2 + core, attn)

    def in_z(s):
        return (dp, x * NZ + lax.rem(z + s, NZ))

    def remote(src, dst, send, recv, device):
        return pltpu.make_async_remote_copy(
            src_ref=src, dst_ref=dst, send_sem=send, recv_sem=recv,
            device_id=device, device_id_type=pl.DeviceIdType.MESH,
        )

    def arrived(ref, sem):
        pltpu.make_async_copy(ref, ref, sem).wait()

    barrier = pltpu.get_barrier_semaphore()

    def greet(device):
        pl.semaphore_signal(barrier, inc=1, device_id=device, device_id_type=pl.DeviceIdType.MESH)

    greet(right)
    greet(left)

    def greet_all(s, carry):
        greet(in_team(s))
        greet(in_y(s))
        greet(in_z(s))
        return carry

    lax.fori_loop(1, 8, greet_all, 0)

    for g in range(HEADS):
        kv[g, 0, 0] = k_ref[:, g * DH:(g + 1) * DH]
        kv[g, 0, 1] = v_ref[:, g * DH:(g + 1) * DH]

    query_pos = attn * TOK + lax.broadcasted_iota(jnp.int32, (1, TOK), 1)
    first = jnp.zeros((1, TOK), jnp.int32)
    bound = jnp.int32(0)
    for c in range(doc_ref.shape[1]):
        bound = bound + doc_ref[0, c]
        first = jnp.where(query_pos >= bound, bound, first)
    for o in range(SPAN + 1):
        key_pos = (attn - o) * TOK + lax.broadcasted_iota(jnp.int32, (TOK, TOK), 0)
        seen = (key_pos >= first) & (key_pos <= query_pos)
        bias[o * TOK:(o + 1) * TOK] = jnp.where(seen, 0.0, HIDDEN)

    pl.semaphore_wait(barrier, 2 + 7 * 3)

    def at(t, delay, body):
        g = t - delay
        pl.when((g >= 0) & (g < HEADS))(lambda: body(jnp.clip(g, 0, HEADS - 1)))

    def pass_in(g, o):
        return remote(kv.at[g, o], kv.at[g, o + 1], in_s.at[g, o], in_r.at[g, o], right)

    def pass_out(g, o):
        return remote(osend.at[g, o], orecv.at[g, o], out_s.at[g, o], out_r.at[g, o], left)

    def share_x(r):
        return remote(x_ref.at[:, in_slot(r)], xin.at[r], x_s.at[r], x_r.at[r], in_team(r))

    def in_slot(r):
        return lax.rem(core + r // NX, 2) * NX + lax.rem(x + lax.rem(r, NX), NX)

    own_x = pltpu.make_async_copy(x_ref.at[:, in_slot(0)], xin.at[0], x_own)

    def do_in0(g):
        pass_in(g, 0).start()

    def do_in1(g):
        pass_in(g, 0).wait_recv()
        pass_in(g, 1).start()

    def do_in2(g):
        pass_in(g, 1).wait_recv()
        pass_in(g, 2).start()

    def nt(a, b):
        return lax.dot_general(a, b, (((1,), (1,)), ((), ())), preferred_element_type=f32)

    def do_att(g):
        pass_in(g, 2).wait_recv()
        keys = kv[g, :, 0].reshape(4 * TOK, DH)
        values = kv[g, :, 1].reshape(4 * TOK, DH)
        group = pl.ds(pl.multiple_of(g * MEMBERS * DH, DH), MEMBERS * DH)

        def member(j, carry):
            cols = pl.ds(pl.multiple_of((g * MEMBERS + j) * DH, DH), DH)
            scores = nt(keys, q_ref[:, cols]) + bias[...]
            dprobs = nt(values, og_ref[:, cols])
            top = jnp.max(scores, axis=0, keepdims=True)
            weights = jnp.exp2((scores - top) * (LOG2E * DH ** -0.5))
            p = weights * (1.0 / jnp.sum(weights, axis=0, keepdims=True))
            delta = jnp.sum(p * dprobs, axis=0, keepdims=True)
            spot = pl.ds(pl.multiple_of(j * TOK, TOK), TOK)
            probs[:, spot] = p.astype(bf16)
            dscores[:, spot] = (p * (dprobs - delta)).astype(bf16)
            return carry

        lax.fori_loop(0, MEMBERS, member, 0)
        ds = dscores[...]

        def stacked(ref):
            wide = ref[:, group]
            return jnp.concatenate([wide[:, j * DH:(j + 1) * DH] for j in range(MEMBERS)], axis=0)

        dk = jnp.dot(ds, stacked(q_ref), preferred_element_type=f32) * (DH ** -0.5)
        dv = jnp.dot(probs[...], stacked(og_ref), preferred_element_type=f32)
        for o in range(SPAN + 1):
            parts[g, o, :, :DH] = dk[o * TOK:(o + 1) * TOK]
            parts[g, o, :, DH:] = dv[o * TOK:(o + 1) * TOK]
        osend[g, 0] = parts[g, SPAN].astype(bf16)
        pass_out(g, 0).start()
        dqt = jnp.dot(keys.T, ds, preferred_element_type=f32) * (DH ** -0.5)
        dq_ref[:, group] = jnp.concatenate(
            [dqt[:, j * TOK:(j + 1) * TOK].T for j in range(MEMBERS)], axis=1
        ).astype(bf16)

    def do_out2(g):
        pass_out(g, 0).wait_recv()
        osend[g, 1] = (orecv[g, 0].astype(f32) + parts[g, 2]).astype(bf16)
        pass_out(g, 1).start()

    def do_out3(g):
        pass_out(g, 1).wait_recv()
        osend[g, 2] = (orecv[g, 1].astype(f32) + parts[g, 1]).astype(bf16)
        pass_out(g, 2).start()

    def share_rows(g, r):
        return remote(rows.at[g, 0], rows.at[g, r], ag_s.at[g], ag_r.at[g], in_team(r))

    def do_out4(g):
        pass_out(g, 2).wait_recv()
        rows[g, 0] = (orecv[g, 2].astype(f32) + parts[g, 0]).astype(bf16)

        def send(r, carry):
            share_rows(g, r).start()
            return carry

        lax.fori_loop(1, 8, send, 0)

    def share_y(g, s):
        return remote(
            wsend.at[g, lax.rem(y + s, NY)], yrecv.at[g, s - 1], y_s.at[g], y_r.at[g], in_y(s)
        )

    def do_mul(g):
        arrived(rows.at[g, pl.ds(1, 7)], ag_r.at[g])
        taken = jnp.concatenate(
            [xin[r].reshape(NY * 64, TOK) for r in range(8)], axis=1
        )
        out = jnp.dot(taken, rows[g].reshape(8 * TOK, 2 * DH), preferred_element_type=f32)
        wsend[g] = out.astype(bf16).reshape(NY, 64, 2 * DH)

        def send(s, carry):
            share_y(g, s).start()
            return carry

        lax.fori_loop(1, NY, send, 0)

    def share_z(g, s):
        return remote(
            zsend.at[g, lax.rem(z + s, NZ)], zrecv.at[g, s - 1], z_s.at[g], z_r.at[g], in_z(s)
        )

    def do_sumy(g):
        arrived(yrecv.at[g], y_r.at[g])
        total = wsend[g, y].astype(f32)
        for s in range(NY - 1):
            total = total + yrecv[g, s].astype(f32)
        zsend[g] = total.reshape(NZ, 8, 2 * DH)

        def send(s, carry):
            share_z(g, s).start()
            return carry

        lax.fori_loop(1, NZ, send, 0)

    norm = (NX * NY * NZ * 2 * TOK) ** -0.5

    def do_sumz(g):
        arrived(zrecv.at[g], z_r.at[g])
        total = zsend[g, z]
        for s in range(NZ - 1):
            total = total + zrecv[g, s]
        total = total * norm
        w_ref[:, pl.ds(pl.multiple_of(g * DH, DH), DH)] = total[:, :DH]
        w_ref[:, pl.ds(pl.multiple_of((HEADS + g) * DH, DH), DH)] = total[:, DH:]

    def step(t, carry):
        at(t, IN0, do_in0)

        @pl.when(t == 0)
        def _():
            own_x.start()

            def send(r, inner):
                share_x(r).start()
                return inner

            lax.fori_loop(1, 8, send, 0)

        at(t, IN1, do_in1)
        at(t, IN2, do_in2)
        at(t, SUMZ, do_sumz)
        at(t, SUMY, do_sumy)

        @pl.when(t == MUL)
        def _():
            own_x.wait()

            def receive(r, inner):
                share_x(r).wait_recv()
                return inner

            lax.fori_loop(1, 8, receive, 0)

        at(t, MUL, do_mul)
        at(t, OUT4, do_out4)
        at(t, OUT3, do_out3)
        at(t, OUT2, do_out2)
        at(t, ATT, do_att)
        return carry

    lax.fori_loop(0, STEPS, step, 0)

    def sent_x(r, carry):
        share_x(r).wait_send()
        return carry

    lax.fori_loop(1, 8, sent_x, 0)

    def sent(g, carry):
        for o in range(SPAN):
            pass_in(g, o).wait_send()
            pass_out(g, o).wait_send()
        arrived(rows.at[g, pl.ds(1, 7)], ag_s.at[g])
        arrived(yrecv.at[g], y_s.at[g])
        arrived(zrecv.at[g], z_s.at[g])
        return carry

    lax.fori_loop(0, HEADS, sent, 0)


def shards(query_states, key_states, value_states, out_grad, doc_lengths, layer_inputs):
    rows_dev, width = query_states.shape
    columns = 2 * key_states.shape[1]
    team = 2 * NX
    by_row = layer_inputs.reshape(NY, team, layer_inputs.shape[0] // (NY * team), rows_dev)
    bf16, f32 = jnp.bfloat16, jnp.float32
    vmem = pl.BlockSpec(memory_space=pltpu.VMEM)
    dma = pltpu.SemaphoreType.DMA
    return pl.pallas_call(
        kernel,
        out_shape=(
            jax.ShapeDtypeStruct((rows_dev, width), bf16),
            jax.ShapeDtypeStruct((8, columns), f32),
        ),
        in_specs=[
            pl.BlockSpec(memory_space=pltpu.SMEM), vmem, vmem, vmem, vmem,
            pl.BlockSpec(memory_space=pl.ANY),
        ],
        out_specs=(vmem, vmem),
        scratch_shapes=[
            pltpu.VMEM((HEADS, SPAN + 1, 2, TOK, DH), bf16),
            pltpu.VMEM((4 * TOK, TOK), f32),
            pltpu.VMEM((4 * TOK, MEMBERS * TOK), bf16),
            pltpu.VMEM((4 * TOK, MEMBERS * TOK), bf16),
            pltpu.VMEM((HEADS, SPAN + 1, TOK, 2 * DH), f32),
            pltpu.VMEM((HEADS, SPAN, TOK, 2 * DH), bf16),
            pltpu.VMEM((HEADS, SPAN, TOK, 2 * DH), bf16),
            pltpu.VMEM((HEADS, 8, TOK, 2 * DH), bf16),
            pltpu.VMEM((8, NY, 64, TOK), bf16),
            pltpu.VMEM((HEADS, NY, 64, 2 * DH), bf16),
            pltpu.VMEM((HEADS, NY - 1, 64, 2 * DH), bf16),
            pltpu.VMEM((HEADS, NZ, 8, 2 * DH), f32),
            pltpu.VMEM((HEADS, NZ - 1, 8, 2 * DH), f32),
            dma((HEADS, SPAN)), dma((HEADS, SPAN)),
            dma((HEADS, SPAN)), dma((HEADS, SPAN)),
            dma((8,)), dma((8,)), dma,
            dma((HEADS,)), dma((HEADS,)),
            dma((HEADS,)), dma((HEADS,)),
            dma((HEADS,)), dma((HEADS,)),
        ],
        compiler_params=pltpu.CompilerParams(
            collective_id=0, has_side_effects=True, vmem_limit_bytes=44 << 20
        ),
        name="attention_and_weight_grad",
    )(doc_lengths, query_states, key_states, value_states, out_grad, by_row)


def solution(mesh):
    whole = P(("dp", "attn"), None)
    return jax.shard_map(
        shards,
        mesh=mesh,
        in_specs=(whole, whole, whole, whole, P("dp", None), P(None, ("dp", "attn"))),
        out_specs=(whole, whole),
        check_vma=False,
    )
```

```python
import functools

import jax
import jax.numpy as jnp
from jax import lax
from jax.experimental import pallas as pl
from jax.experimental.pallas import tpu as pltpu
from jax.sharding import PartitionSpec as P

DH = 128
SPAN = 3
NX, NY, NZ = 4, 8, 8
MEMBERS = 8
HEADS = 4
TOK = 128
LOG2E = 1.4426950408889634
HIDDEN = -1e30

IN0, IN1, IN2, ATT, OUT2, OUT3, OUT4, MUL, SUMY, SUMZ = 0, 1, 2, 3, 5, 6, 7, 9, 12, 14
STEPS = 2 * HEADS - 1 + SUMZ
HALF = MEMBERS // 2


def kernel(
    doc_hbm, q_hbm, k_hbm, v_hbm, og_hbm, x_ref, dq_hbm, w_ref,
    doc_ref, q_ref, og_ref, dq_ref, kv, bias, parts, osend, orecv, rows, xin, wsend, yrecv, zsend, zrecv,
    load_s, kv_s, dq_s, in_s, in_r, out_s, out_r, x_s, x_r, x_own, ag_s, ag_r, y_s, y_r, z_s, z_r,
):
    f32, bf16 = jnp.float32, jnp.bfloat16
    attn, dp = lax.axis_index("attn"), lax.axis_index("dp")
    x, z = attn // NZ, lax.rem(attn, NZ)
    y, core = dp // 2, lax.rem(dp, 2)
    right = (dp, lax.rem(attn + 1, NX * NZ))
    left = (dp, lax.rem(attn + NX * NZ - 1, NX * NZ))

    def in_team(r):
        c = lax.rem(core + r // NX, 2)
        return (y * 2 + c, lax.rem(x + lax.rem(r, NX), NX) * NZ + z)

    def in_y(s):
        return (lax.rem(y + s, NY) * 2 + core, attn)

    def in_z(s):
        return (dp, x * NZ + lax.rem(z + s, NZ))

    def remote(src, dst, send, recv, device):
        return pltpu.make_async_remote_copy(
            src_ref=src, dst_ref=dst, send_sem=send, recv_sem=recv,
            device_id=device, device_id_type=pl.DeviceIdType.MESH,
        )

    def arrived(ref, sem):
        pltpu.make_async_copy(ref, ref, sem).wait()

    loads = [
        pltpu.make_async_copy(src, dst, load_s.at[i])
        for i, (src, dst) in enumerate(((doc_hbm, doc_ref), (q_hbm, q_ref), (og_hbm, og_ref)))
    ]

    def own_kv(g):
        cols = pl.ds(pl.multiple_of(g * DH, DH), DH)
        return [
            pltpu.make_async_copy(src.at[:, cols], kv.at[g, 0, i], kv_s.at[g, i])
            for i, src in enumerate((k_hbm, v_hbm))
        ]

    loads[0].start()
    for g in range(HEADS):
        for copy in own_kv(g):
            copy.start()
    loads[1].start()
    loads[2].start()

    barrier = pltpu.get_barrier_semaphore()

    def greet(device):
        pl.semaphore_signal(barrier, inc=1, device_id=device, device_id_type=pl.DeviceIdType.MESH)

    greet(right)
    greet(left)

    def greet_all(s, carry):
        greet(in_team(s))
        greet(in_y(s))
        greet(in_z(s))
        return carry

    lax.fori_loop(1, 8, greet_all, 0)

    loads[0].wait()
    query_pos = attn * TOK + lax.broadcasted_iota(jnp.int32, (1, TOK), 1)
    first = jnp.zeros((1, TOK), jnp.int32)
    bound = jnp.int32(0)
    for c in range(doc_ref.shape[1]):
        bound = bound + doc_ref[0, c]
        first = jnp.where(query_pos >= bound, bound, first)
    for o in range(SPAN + 1):
        key_pos = (attn - o) * TOK + lax.broadcasted_iota(jnp.int32, (TOK, TOK), 0)
        seen = (key_pos >= first) & (key_pos <= query_pos)
        bias[o * TOK:(o + 1) * TOK] = jnp.where(seen, 0.0, HIDDEN)

    pl.semaphore_wait(barrier, 2 + 7 * 3)

    def at(t, delay, body):
        late = t - delay
        due = (late >= 0) & (late < 2 * HEADS) & (lax.rem(late + 2, 2) == 0)
        pl.when(due)(lambda: body(jnp.clip(late // 2, 0, HEADS - 1)))

    def pass_in(g, o):
        return remote(kv.at[g, o], kv.at[g, o + 1], in_s.at[g, o], in_r.at[g, o], right)

    def pass_out(g, o):
        return remote(osend.at[g, o], orecv.at[g, o], out_s.at[g, o], out_r.at[g, o], left)

    def share_x(r):
        return remote(x_ref.at[:, in_slot(r)], xin.at[r], x_s.at[r], x_r.at[r], in_team(r))

    def in_slot(r):
        return lax.rem(core + r // NX, 2) * NX + lax.rem(x + lax.rem(r, NX), NX)

    own_x = pltpu.make_async_copy(x_ref.at[:, in_slot(0)], xin.at[0], x_own)

    def do_in0(g):
        for copy in own_kv(g):
            copy.wait()
        pass_in(g, 0).start()

    def do_in1(g):
        pass_in(g, 0).wait_recv()
        pass_in(g, 1).start()

    def do_in2(g):
        pass_in(g, 1).wait_recv()
        pass_in(g, 2).start()

    def nt(a, b):
        return lax.dot_general(a, b, (((1,), (1,)), ((), ())), preferred_element_type=f32)

    def leave_dq(g, half):
        cols = pl.ds(pl.multiple_of((g * MEMBERS + half * HALF) * DH, HALF * DH), HALF * DH)
        return pltpu.make_async_copy(dq_ref.at[:, cols], dq_hbm.at[:, cols], dq_s.at[g, half])

    def do_att(g, half):
        keys = kv[g, :, 0].reshape(4 * TOK, DH)
        values = kv[g, :, 1].reshape(4 * TOK, DH)
        base = (g * MEMBERS + half * HALF) * DH
        group = pl.ds(pl.multiple_of(base, HALF * DH), HALF * DH)

        def heads_of(ref):
            wide = ref[:, group]
            return [wide[:, j * DH:(j + 1) * DH] for j in range(HALF)]

        queries, grads = heads_of(q_ref), heads_of(og_ref)
        low_probs, dscores = [], []
        for j in range(HALF):
            scores = nt(keys, queries[j]) + bias[...]
            dprobs = nt(values, grads[j])
            top = jnp.max(scores, axis=0, keepdims=True)
            weights = jnp.exp2((scores - top) * (LOG2E * DH ** -0.5))
            p = weights * (1.0 / jnp.sum(weights, axis=0, keepdims=True))
            delta = jnp.sum(p * dprobs, axis=0, keepdims=True)
            low_probs.append(p.astype(bf16))
            dscores.append((p * (dprobs - delta)).astype(bf16))
        ds = jnp.concatenate(dscores, axis=1)
        dk = jnp.dot(ds, jnp.concatenate(queries, axis=0), preferred_element_type=f32)
        dv = jnp.dot(
            jnp.concatenate(low_probs, axis=1), jnp.concatenate(grads, axis=0),
            preferred_element_type=f32,
        )
        new = jnp.concatenate([dk * (DH ** -0.5), dv], axis=1).reshape(SPAN + 1, TOK, 2 * DH)
        dqt = jnp.dot(keys.T, ds, preferred_element_type=f32) * (DH ** -0.5)
        dq_ref[:, group] = jnp.concatenate(
            [dqt[:, j * TOK:(j + 1) * TOK].T for j in range(HALF)], axis=1
        ).astype(bf16)
        leave_dq(g, half).start()

        @pl.when(half == 0)
        def _():
            parts[g] = new

        @pl.when(half == 1)
        def _():
            total = parts[g] + new
            parts[g] = total
            osend[g, 0] = total[SPAN].astype(bf16)
            pass_out(g, 0).start()

    def do_out2(g):
        pass_out(g, 0).wait_recv()
        osend[g, 1] = (orecv[g, 0].astype(f32) + parts[g, 2]).astype(bf16)
        pass_out(g, 1).start()

    def do_out3(g):
        pass_out(g, 1).wait_recv()
        osend[g, 2] = (orecv[g, 1].astype(f32) + parts[g, 1]).astype(bf16)
        pass_out(g, 2).start()

    def share_rows(g, r):
        return remote(rows.at[g, 0], rows.at[g, r], ag_s.at[g], ag_r.at[g], in_team(r))

    def do_out4(g):
        pass_out(g, 2).wait_recv()
        rows[g, 0] = (orecv[g, 2].astype(f32) + parts[g, 0]).astype(bf16)

        def send(r, carry):
            share_rows(g, r).start()
            return carry

        lax.fori_loop(1, 8, send, 0)

    def share_y(g, s):
        return remote(
            wsend.at[g, lax.rem(y + s, NY)], yrecv.at[g, s - 1], y_s.at[g], y_r.at[g], in_y(s)
        )

    def do_mul(g):
        arrived(rows.at[g, pl.ds(1, 7)], ag_r.at[g])
        taken = jnp.concatenate(
            [xin[r].reshape(NY * 64, TOK) for r in range(8)], axis=1
        )
        out = jnp.dot(taken, rows[g].reshape(8 * TOK, 2 * DH), preferred_element_type=f32)
        wsend[g] = out.astype(bf16).reshape(NY, 64, 2 * DH)

        def send(s, carry):
            share_y(g, s).start()
            return carry

        lax.fori_loop(1, NY, send, 0)

    def share_z(g, s):
        return remote(
            zsend.at[g, lax.rem(z + s, NZ)], zrecv.at[g, s - 1], z_s.at[g], z_r.at[g], in_z(s)
        )

    def do_sumy(g):
        arrived(yrecv.at[g], y_r.at[g])
        total = wsend[g, y].astype(f32)
        for s in range(NY - 1):
            total = total + yrecv[g, s].astype(f32)
        zsend[g] = total.reshape(NZ, 8, 2 * DH)

        def send(s, carry):
            share_z(g, s).start()
            return carry

        lax.fori_loop(1, NZ, send, 0)

    norm = (NX * NY * NZ * 2 * TOK) ** -0.5

    def do_sumz(g):
        arrived(zrecv.at[g], z_r.at[g])
        total = zsend[g, z]
        for s in range(NZ - 1):
            total = total + zrecv[g, s]
        total = total * norm
        w_ref[:, pl.ds(pl.multiple_of(g * DH, DH), DH)] = total[:, :DH]
        w_ref[:, pl.ds(pl.multiple_of((HEADS + g) * DH, DH), DH)] = total[:, DH:]

    def step(t, carry):
        at(t, IN0, do_in0)

        @pl.when(t == 0)
        def _():
            own_x.start()

            def send(r, inner):
                share_x(r).start()
                return inner

            lax.fori_loop(1, 8, send, 0)

        at(t, IN1, do_in1)
        at(t, IN2, do_in2)
        at(t, OUT2, do_out2)
        at(t, OUT3, do_out3)
        at(t, OUT4, do_out4)

        @pl.when(t == MUL)
        def _():
            own_x.wait()

            def receive(r, inner):
                share_x(r).wait_recv()
                return inner

            lax.fori_loop(1, 8, receive, 0)

        at(t, MUL, do_mul)
        at(t, SUMY, do_sumy)
        at(t, SUMZ, do_sumz)

        @pl.when(t == ATT)
        def _():
            loads[1].wait()
            loads[2].wait()

        late = t - ATT

        @pl.when((late >= 0) & (late < 2 * HEADS))
        def _():
            g = jnp.clip(late // 2, 0, HEADS - 1)
            half = lax.rem(late + 2, 2)

            @pl.when(half == 0)
            def _():
                pass_in(g, 2).wait_recv()

            do_att(g, half)

        return carry

    lax.fori_loop(0, STEPS, step, 0)

    def sent_x(r, carry):
        share_x(r).wait_send()
        return carry

    lax.fori_loop(1, 8, sent_x, 0)

    def sent(g, carry):
        for o in range(SPAN):
            pass_in(g, o).wait_send()
            pass_out(g, o).wait_send()
        arrived(rows.at[g, pl.ds(1, 7)], ag_s.at[g])
        arrived(yrecv.at[g], y_s.at[g])
        arrived(zrecv.at[g], z_s.at[g])
        leave_dq(g, 0).wait()
        leave_dq(g, 1).wait()
        return carry

    lax.fori_loop(0, HEADS, sent, 0)


def shards(query_states, key_states, value_states, out_grad, doc_lengths, layer_inputs):
    rows_dev, width = query_states.shape
    columns = 2 * key_states.shape[1]
    team = 2 * NX
    by_row = layer_inputs.reshape(NY, team, layer_inputs.shape[0] // (NY * team), rows_dev)
    bf16, f32 = jnp.bfloat16, jnp.float32
    vmem = pl.BlockSpec(memory_space=pltpu.VMEM)
    dma = pltpu.SemaphoreType.DMA
    return pl.pallas_call(
        kernel,
        out_shape=(
            jax.ShapeDtypeStruct((rows_dev, width), bf16),
            jax.ShapeDtypeStruct((8, columns), f32),
        ),
        in_specs=[pl.BlockSpec(memory_space=pltpu.HBM)] * 6,
        out_specs=(pl.BlockSpec(memory_space=pltpu.HBM), vmem),
        scratch_shapes=[
            pltpu.SMEM(doc_lengths.shape, jnp.int32),
            pltpu.VMEM((rows_dev, width), bf16),
            pltpu.VMEM((rows_dev, width), bf16),
            pltpu.VMEM((rows_dev, width), bf16),
            pltpu.VMEM((HEADS, SPAN + 1, 2, TOK, DH), bf16),
            pltpu.VMEM((4 * TOK, TOK), f32),
            pltpu.VMEM((HEADS, SPAN + 1, TOK, 2 * DH), f32),
            pltpu.VMEM((HEADS, SPAN, TOK, 2 * DH), bf16),
            pltpu.VMEM((HEADS, SPAN, TOK, 2 * DH), bf16),
            pltpu.VMEM((HEADS, 8, TOK, 2 * DH), bf16),
            pltpu.VMEM((8, NY, 64, TOK), bf16),
            pltpu.VMEM((HEADS, NY, 64, 2 * DH), bf16),
            pltpu.VMEM((HEADS, NY - 1, 64, 2 * DH), bf16),
            pltpu.VMEM((HEADS, NZ, 8, 2 * DH), f32),
            pltpu.VMEM((HEADS, NZ - 1, 8, 2 * DH), f32),
            dma((3,)), dma((HEADS, 2)), dma((HEADS, 2)),
            dma((HEADS, SPAN)), dma((HEADS, SPAN)),
            dma((HEADS, SPAN)), dma((HEADS, SPAN)),
            dma((8,)), dma((8,)), dma,
            dma((HEADS,)), dma((HEADS,)),
            dma((HEADS,)), dma((HEADS,)),
            dma((HEADS,)), dma((HEADS,)),
        ],
        compiler_params=pltpu.CompilerParams(
            collective_id=0, has_side_effects=True, vmem_limit_bytes=62 << 20
        ),
        name="attention_and_weight_grad",
    )(doc_lengths, query_states, key_states, value_states, out_grad, by_row)


def solution(mesh):
    whole = P(("dp", "attn"), None)
    return jax.shard_map(
        shards,
        mesh=mesh,
        in_specs=(whole, whole, whole, whole, P("dp", None), P(None, ("dp", "attn"))),
        out_specs=(whole, whole),
        check_vma=False,
    )
```

```python
import functools

import jax
import jax.numpy as jnp
from jax import lax
from jax.experimental import pallas as pl
from jax.experimental.pallas import tpu as pltpu
from jax.sharding import PartitionSpec as P

DH = 128
SPAN = 3
NX, NY, NZ = 4, 8, 8
MEMBERS = 8
HEADS = 4
TOK = 128
LOG2E = 1.4426950408889634
HIDDEN = -1e30

IN1, IN2, SEND_X, ATT = 0, 1, 1, 3
OUT2, OUT3, OUT4, MATE, MUL, SUMY, SUMZ = 7, 9, 11, 13, 15, 19, 22
STEPS = 2 * HEADS - 1 + SUMZ
HALF = MEMBERS // 2


def kernel(
    doc_hbm, q_hbm, k_hbm, v_hbm, og_hbm, x_ref, dq_hbm, w_ref,
    doc_ref, q_ref, og_ref, dq_ref, kv, bias, parts, osend, orecv, rows, xin, ksend, krecv, vsend, vrecv,
    ksum, klast, vsum, vlast,
    load_s, kv_s, dq_s, in_s, in_r, out_s, out_r, x_s, x_r, x_own, ag_s, ag_r, mate_s, mate_r, y_s, y_r, z_s, z_r,
    y2_s, y2_r, z2_s, z2_r,
):
    f32, bf16 = jnp.float32, jnp.bfloat16
    attn, dp = lax.axis_index("attn"), lax.axis_index("dp")
    x, z = attn // NZ, lax.rem(attn, NZ)
    y, core = dp // 2, lax.rem(dp, 2)
    right = (dp, lax.rem(attn + 1, NX * NZ))
    left = (dp, lax.rem(attn + NX * NZ - 1, NX * NZ))

    def in_team(r):
        c = lax.rem(core + r // NX, 2)
        return (y * 2 + c, lax.rem(x + lax.rem(r, NX), NX) * NZ + z)

    def in_y(s):
        return (lax.rem(y + s, NY) * 2 + core, attn)

    def in_z(s):
        return (dp, x * NZ + lax.rem(z + s, NZ))

    def remote(src, dst, send, recv, device):
        return pltpu.make_async_remote_copy(
            src_ref=src, dst_ref=dst, send_sem=send, recv_sem=recv,
            device_id=device, device_id_type=pl.DeviceIdType.MESH,
        )

    def arrived(ref, sem):
        pltpu.make_async_copy(ref, ref, sem).wait()

    loads = [
        pltpu.make_async_copy(src, dst, load_s.at[i])
        for i, (src, dst) in enumerate(((doc_hbm, doc_ref), (q_hbm, q_ref), (og_hbm, og_ref)))
    ]

    def own_kv(g):
        cols = pl.ds(pl.multiple_of(g * DH, DH), DH)
        return [
            pltpu.make_async_copy(src.at[:, cols], kv.at[g, 0, i], kv_s.at[g, i])
            for i, src in enumerate((k_hbm, v_hbm))
        ]

    loads[0].start()
    for g in range(HEADS):
        for copy in own_kv(g):
            copy.start()
    loads[1].start()
    loads[2].start()

    barrier = pltpu.get_barrier_semaphore()

    def greet(device):
        pl.semaphore_signal(barrier, inc=1, device_id=device, device_id_type=pl.DeviceIdType.MESH)

    greet(right)
    greet(left)

    def greet_all(s, carry):
        greet(in_team(s))
        greet(in_y(s))
        greet(in_z(s))
        return carry

    lax.fori_loop(1, 8, greet_all, 0)

    loads[0].wait()
    query_pos = attn * TOK + lax.broadcasted_iota(jnp.int32, (1, TOK), 1)
    first = jnp.zeros((1, TOK), jnp.int32)
    bound = jnp.int32(0)
    for c in range(doc_ref.shape[1]):
        bound = bound + doc_ref[0, c]
        first = jnp.where(query_pos >= bound, bound, first)
    for o in range(SPAN + 1):
        key_pos = (attn - o) * TOK + lax.broadcasted_iota(jnp.int32, (TOK, TOK), 0)
        seen = (key_pos >= first) & (key_pos <= query_pos)
        bias[o * TOK:(o + 1) * TOK] = jnp.where(seen, 0.0, HIDDEN)

    pl.semaphore_wait(barrier, 2 + 7 * 3)

    def at(t, delay, body, every=2):
        late = t - delay
        due = (late >= 0) & (late < every * HEADS) & (lax.rem(late + 2, every) == 0)
        pl.when(due)(lambda: body(jnp.clip(late // every, 0, HEADS - 1)))

    def pass_in(g, o):
        return remote(kv.at[g, o], kv.at[g, o + 1], in_s.at[g, o], in_r.at[g, o], right)

    def pass_out(g, o):
        return remote(osend.at[g, o], orecv.at[g, o], out_s.at[g, o], out_r.at[g, o], left)

    def share_x(r):
        return remote(x_ref.at[:, in_slot(r)], xin.at[r], x_s.at[r], x_r.at[r], in_team(r))

    def in_slot(r):
        return lax.rem(core + r // NX, 2) * NX + lax.rem(x + lax.rem(r, NX), NX)

    own_x = pltpu.make_async_copy(x_ref.at[:, in_slot(0)], xin.at[0], x_own)

    def do_in0(g):
        for copy in own_kv(g):
            copy.wait()
        pass_in(g, 0).start()

    def do_in1(g):
        pass_in(g, 0).wait_recv()
        pass_in(g, 1).start()

    def do_in2(g):
        pass_in(g, 1).wait_recv()
        pass_in(g, 2).start()

    def nt(a, b):
        return lax.dot_general(a, b, (((1,), (1,)), ((), ())), preferred_element_type=f32)

    def leave_dq(g, half):
        cols = pl.ds(pl.multiple_of((g * MEMBERS + half * HALF) * DH, HALF * DH), HALF * DH)
        return pltpu.make_async_copy(dq_ref.at[:, cols], dq_hbm.at[:, cols], dq_s.at[g, half])

    def do_att(g, half):
        keys = kv[g, :, 0].reshape(4 * TOK, DH)
        values = kv[g, :, 1].reshape(4 * TOK, DH)
        base = (g * MEMBERS + half * HALF) * DH
        group = pl.ds(pl.multiple_of(base, HALF * DH), HALF * DH)

        def heads_of(ref):
            wide = ref[:, group]
            return [wide[:, j * DH:(j + 1) * DH] for j in range(HALF)]

        queries, grads = heads_of(q_ref), heads_of(og_ref)
        low_probs, dscores = [], []
        for j in range(HALF):
            scores = nt(keys, queries[j]) + bias[...]
            dprobs = nt(values, grads[j])
            top = jnp.max(scores, axis=0, keepdims=True)
            weights = jnp.exp2((scores - top) * (LOG2E * DH ** -0.5))
            p = weights * (1.0 / jnp.sum(weights, axis=0, keepdims=True))
            delta = jnp.sum(p * dprobs, axis=0, keepdims=True)
            low_probs.append(p.astype(bf16))
            dscores.append((p * (dprobs - delta)).astype(bf16))
        ds = jnp.concatenate(dscores, axis=1)
        dk = jnp.dot(ds, jnp.concatenate(queries, axis=0), preferred_element_type=f32)
        dv = jnp.dot(
            jnp.concatenate(low_probs, axis=1), jnp.concatenate(grads, axis=0),
            preferred_element_type=f32,
        )
        new = jnp.concatenate([dk * (DH ** -0.5), dv], axis=1).reshape(SPAN + 1, TOK, 2 * DH)
        dqt = jnp.dot(keys.T, ds, preferred_element_type=f32) * (DH ** -0.5)
        dq_ref[:, group] = jnp.concatenate(
            [dqt[:, j * TOK:(j + 1) * TOK].T for j in range(HALF)], axis=1
        ).astype(bf16)
        leave_dq(g, half).start()

        @pl.when(half == 0)
        def _():
            parts[g] = new

        @pl.when(half == 1)
        def _():
            total = parts[g] + new
            parts[g] = total
            osend[g, 0] = total[SPAN].astype(bf16)
            pass_out(g, 0).start()

    def do_out2(g):
        pass_out(g, 0).wait_recv()
        osend[g, 1] = (orecv[g, 0].astype(f32) + parts[g, 2]).astype(bf16)
        pass_out(g, 1).start()

    def do_out3(g):
        pass_out(g, 1).wait_recv()
        osend[g, 2] = (orecv[g, 1].astype(f32) + parts[g, 1]).astype(bf16)
        pass_out(g, 2).start()

    def share_rows(g, r):
        return remote(rows.at[g, 0], rows.at[g, r], ag_s.at[g], ag_r.at[g, r], in_team(r))

    def share_mate(g):
        return remote(
            rows.at[g, pl.ds(1, NX - 1)], rows.at[g, pl.ds(NX + 1, NX - 1)],
            mate_s.at[g], mate_r.at[g], in_team(NX),
        )

    def do_mate(g):
        def receive(r, carry):
            share_rows(g, r).wait_recv()
            return carry

        lax.fori_loop(1, NX, receive, 0)
        share_mate(g).start()

    def do_out4(g):
        pass_out(g, 2).wait_recv()
        rows[g, 0] = (orecv[g, 2].astype(f32) + parts[g, 0]).astype(bf16)

        def send(r, carry):
            share_rows(g, r).start()
            return carry

        lax.fori_loop(1, NX + 1, send, 0)

    def share_y(g, s):
        return remote(
            ksend.at[g, lax.rem(y + s, NY)], krecv.at[g, s - 1], y_s.at[g], y_r.at[g], in_y(s)
        )

    def share_z(g, s):
        return remote(
            vsend.at[g, lax.rem(z + s, NZ)], vrecv.at[g, s - 1], z_s.at[g], z_r.at[g], in_z(s)
        )

    def last_z(g, s):
        return remote(
            ksum.at[g, lax.rem(z + s, NZ)], klast.at[g, s - 1], z2_s.at[g], z2_r.at[g], in_z(s)
        )

    def last_y(g, s):
        return remote(
            vsum.at[g, lax.rem(y + s, NY)], vlast.at[g, s - 1], y2_s.at[g], y2_r.at[g], in_y(s)
        )

    def do_mul(g):
        share_rows(g, NX).wait_recv()
        share_mate(g).wait_recv()
        taken = jnp.concatenate(
            [xin[r].reshape(NY * 64, TOK) for r in range(8)], axis=1
        )
        out = jnp.dot(taken, rows[g].reshape(8 * TOK, 2 * DH), preferred_element_type=f32)
        ksend[g] = out[:, :DH].astype(bf16).reshape(NY, 64, DH)
        by_z = [out[(i * NZ + k) * 8:(i * NZ + k + 1) * 8, DH:] for k in range(NZ) for i in range(NY)]
        vsend[g] = jnp.concatenate(by_z, axis=0).astype(bf16).reshape(NZ, 64, DH)

        def send(s, carry):
            share_y(g, s).start()
            share_z(g, s).start()
            return carry

        lax.fori_loop(1, NY, send, 0)

    def do_sumy(g):
        arrived(krecv.at[g], y_r.at[g])
        total = ksend[g, y].astype(f32)
        for s in range(NY - 1):
            total = total + krecv[g, s].astype(f32)
        ksum[g] = total.reshape(NZ, 8, DH)
        arrived(vrecv.at[g], z_r.at[g])
        total = vsend[g, z].astype(f32)
        for s in range(NZ - 1):
            total = total + vrecv[g, s].astype(f32)
        vsum[g] = total.reshape(NY, 8, DH)

        def send(s, carry):
            last_z(g, s).start()
            last_y(g, s).start()
            return carry

        lax.fori_loop(1, NZ, send, 0)

    norm = (NX * NY * NZ * 2 * TOK) ** -0.5

    def do_sumz(g):
        arrived(klast.at[g], z2_r.at[g])
        arrived(vlast.at[g], y2_r.at[g])
        key_total, value_total = ksum[g, z], vsum[g, y]
        for s in range(NZ - 1):
            key_total = key_total + klast[g, s]
            value_total = value_total + vlast[g, s]
        w_ref[:, pl.ds(pl.multiple_of(g * DH, DH), DH)] = key_total * norm
        w_ref[:, pl.ds(pl.multiple_of((HEADS + g) * DH, DH), DH)] = value_total * norm

    def step(t, carry):
        at(t, IN1, do_in1, 1)
        at(t, IN2, do_in2, 1)

        @pl.when(t == SEND_X)
        def _():
            own_x.start()

            def send(r, inner):
                share_x(r).start()
                return inner

            lax.fori_loop(1, 8, send, 0)

        at(t, OUT2, do_out2)
        at(t, OUT3, do_out3)
        at(t, OUT4, do_out4)
        at(t, MATE, do_mate)

        @pl.when(t == MUL)
        def _():
            own_x.wait()

            def receive(r, inner):
                share_x(r).wait_recv()
                return inner

            lax.fori_loop(1, 8, receive, 0)

        at(t, MUL, do_mul)
        at(t, SUMY, do_sumy)
        at(t, SUMZ, do_sumz)

        @pl.when(t == ATT)
        def _():
            loads[1].wait()
            loads[2].wait()

        late = t - ATT

        @pl.when((late >= 0) & (late < 2 * HEADS))
        def _():
            g = jnp.clip(late // 2, 0, HEADS - 1)
            half = lax.rem(late + 2, 2)

            @pl.when(half == 0)
            def _():
                pass_in(g, 2).wait_recv()

            do_att(g, half)

        return carry

    def start_in(g, carry):
        do_in0(g)
        return carry

    lax.fori_loop(0, HEADS, start_in, 0)
    lax.fori_loop(0, STEPS, step, 0)

    def sent_x(r, carry):
        share_x(r).wait_send()
        return carry

    lax.fori_loop(1, 8, sent_x, 0)

    def sent(g, carry):
        for o in range(SPAN):
            pass_in(g, o).wait_send()
            pass_out(g, o).wait_send()
        arrived(rows.at[g, pl.ds(1, NX)], ag_s.at[g])
        share_mate(g).wait_send()
        arrived(krecv.at[g], y_s.at[g])
        arrived(vrecv.at[g], z_s.at[g])
        arrived(klast.at[g], z2_s.at[g])
        arrived(vlast.at[g], y2_s.at[g])
        leave_dq(g, 0).wait()
        leave_dq(g, 1).wait()
        return carry

    lax.fori_loop(0, HEADS, sent, 0)


def shards(query_states, key_states, value_states, out_grad, doc_lengths, layer_inputs):
    rows_dev, width = query_states.shape
    columns = 2 * key_states.shape[1]
    team = 2 * NX
    by_row = layer_inputs.reshape(NY, team, layer_inputs.shape[0] // (NY * team), rows_dev)
    bf16, f32 = jnp.bfloat16, jnp.float32
    vmem = pl.BlockSpec(memory_space=pltpu.VMEM)
    dma = pltpu.SemaphoreType.DMA
    return pl.pallas_call(
        kernel,
        out_shape=(
            jax.ShapeDtypeStruct((rows_dev, width), bf16),
            jax.ShapeDtypeStruct((8, columns), f32),
        ),
        in_specs=[pl.BlockSpec(memory_space=pltpu.HBM)] * 6,
        out_specs=(pl.BlockSpec(memory_space=pltpu.HBM), vmem),
        scratch_shapes=[
            pltpu.SMEM(doc_lengths.shape, jnp.int32),
            pltpu.VMEM((rows_dev, width), bf16),
            pltpu.VMEM((rows_dev, width), bf16),
            pltpu.VMEM((rows_dev, width), bf16),
            pltpu.VMEM((HEADS, SPAN + 1, 2, TOK, DH), bf16),
            pltpu.VMEM((4 * TOK, TOK), f32),
            pltpu.VMEM((HEADS, SPAN + 1, TOK, 2 * DH), f32),
            pltpu.VMEM((HEADS, SPAN, TOK, 2 * DH), bf16),
            pltpu.VMEM((HEADS, SPAN, TOK, 2 * DH), bf16),
            pltpu.VMEM((HEADS, 8, TOK, 2 * DH), bf16),
            pltpu.VMEM((8, NY, 64, TOK), bf16),
            pltpu.VMEM((HEADS, NY, 64, DH), bf16),
            pltpu.VMEM((HEADS, NY - 1, 64, DH), bf16),
            pltpu.VMEM((HEADS, NZ, 64, DH), bf16),
            pltpu.VMEM((HEADS, NZ - 1, 64, DH), bf16),
            pltpu.VMEM((HEADS, NZ, 8, DH), f32),
            pltpu.VMEM((HEADS, NZ - 1, 8, DH), f32),
            pltpu.VMEM((HEADS, NY, 8, DH), f32),
            pltpu.VMEM((HEADS, NY - 1, 8, DH), f32),
            dma((3,)), dma((HEADS, 2)), dma((HEADS, 2)),
            dma((HEADS, SPAN)), dma((HEADS, SPAN)),
            dma((HEADS, SPAN)), dma((HEADS, SPAN)),
            dma((8,)), dma((8,)), dma,
            dma((HEADS,)), dma((HEADS, NX + 1)),
            dma((HEADS,)), dma((HEADS,)),
            dma((HEADS,)), dma((HEADS,)),
            dma((HEADS,)), dma((HEADS,)),
            dma((HEADS,)), dma((HEADS,)), dma((HEADS,)), dma((HEADS,)),
        ],
        compiler_params=pltpu.CompilerParams(
            collective_id=0, has_side_effects=True, vmem_limit_bytes=62 << 20
        ),
        name="attention_and_weight_grad",
    )(doc_lengths, query_states, key_states, value_states, out_grad, by_row)


def solution(mesh):
    whole = P(("dp", "attn"), None)
    return jax.shard_map(
        shards,
        mesh=mesh,
        in_specs=(whole, whole, whole, whole, P("dp", None), P(None, ("dp", "attn"))),
        out_specs=(whole, whole),
        check_vma=False,
    )
```

```python
import functools

import jax
import jax.numpy as jnp
from jax import lax
from jax.experimental import pallas as pl
from jax.experimental.pallas import tpu as pltpu
from jax.sharding import PartitionSpec as P

DH = 128
SPAN = 3
NX, NY, NZ = 4, 8, 8
MEMBERS = 8
HEADS = 4
TOK = 128
LOG2E = 1.4426950408889634
HIDDEN = -1e30

IN1, IN2, SEND_X, ATT = 0, 1, 1, 3
OUT2, OUT3, OUT4, MATE, MUL, SUMY, SUMZ = 7, 9, 11, 13, 15, 19, 22
STEPS = 2 * HEADS - 1 + SUMZ
HALF = MEMBERS // 2


def kernel(
    doc_hbm, q_hbm, k_hbm, v_hbm, og_hbm, x_ref, dq_hbm, w_ref,
    doc_ref, q_ref, og_ref, dq_ref, kv, bias, parts, osend, orecv, rows, xin, ksend, krecv, vsend, vrecv,
    ksum, klast, vsum, vlast,
    load_s, kv_s, dq_s, in_s, in_r, out_s, out_r, x_s, x_r, x_own, ag_s, ag_r, mate_s, mate_r, y_s, y_r, z_s, z_r,
    y2_s, y2_r, z2_s, z2_r,
):
    f32, bf16 = jnp.float32, jnp.bfloat16
    attn, dp = lax.axis_index("attn"), lax.axis_index("dp")
    x, z = attn // NZ, lax.rem(attn, NZ)
    y, core = dp // 2, lax.rem(dp, 2)
    right = (dp, lax.rem(attn + 1, NX * NZ))
    left = (dp, lax.rem(attn + NX * NZ - 1, NX * NZ))

    def in_team(r):
        c = lax.rem(core + r // NX, 2)
        return (y * 2 + c, lax.rem(x + lax.rem(r, NX), NX) * NZ + z)

    def in_y(s):
        return (lax.rem(y + s, NY) * 2 + core, attn)

    def in_z(s):
        return (dp, x * NZ + lax.rem(z + s, NZ))

    def remote(src, dst, send, recv, device):
        return pltpu.make_async_remote_copy(
            src_ref=src, dst_ref=dst, send_sem=send, recv_sem=recv,
            device_id=device, device_id_type=pl.DeviceIdType.MESH,
        )

    def arrived(ref, sem):
        pltpu.make_async_copy(ref, ref, sem).wait()

    loads = [
        pltpu.make_async_copy(src, dst, load_s.at[i])
        for i, (src, dst) in enumerate(((doc_hbm, doc_ref), (q_hbm, q_ref), (og_hbm, og_ref)))
    ]

    def own_kv(g):
        cols = pl.ds(pl.multiple_of(g * DH, DH), DH)
        return [
            pltpu.make_async_copy(src.at[:, cols], kv.at[g, 0, i], kv_s.at[g, i])
            for i, src in enumerate((k_hbm, v_hbm))
        ]

    loads[0].start()
    for g in range(HEADS):
        for copy in own_kv(g):
            copy.start()
    loads[1].start()
    loads[2].start()

    barrier = pltpu.get_barrier_semaphore()

    def greet(device):
        pl.semaphore_signal(barrier, inc=1, device_id=device, device_id_type=pl.DeviceIdType.MESH)

    greet(right)
    greet(left)

    def greet_all(s, carry):
        greet(in_team(s))
        greet(in_y(s))
        greet(in_z(s))
        return carry

    lax.fori_loop(1, 8, greet_all, 0)

    loads[0].wait()
    query_pos = attn * TOK + lax.broadcasted_iota(jnp.int32, (1, TOK), 1)
    first = jnp.zeros((1, TOK), jnp.int32)
    bound = jnp.int32(0)
    for c in range(doc_ref.shape[1]):
        bound = bound + doc_ref[0, c]
        first = jnp.where(query_pos >= bound, bound, first)
    for o in range(SPAN + 1):
        key_pos = (attn - o) * TOK + lax.broadcasted_iota(jnp.int32, (TOK, TOK), 0)
        seen = (key_pos >= first) & (key_pos <= query_pos)
        bias[o * TOK:(o + 1) * TOK] = jnp.where(seen, 0.0, HIDDEN)

    pl.semaphore_wait(barrier, 2 + 7 * 3)

    def at(t, delay, body, every=2):
        late = t - delay
        due = (late >= 0) & (late < every * HEADS) & (lax.rem(late + 2, every) == 0)
        pl.when(due)(lambda: body(jnp.clip(late // every, 0, HEADS - 1)))

    def pass_in(g, o):
        return remote(kv.at[g, o], kv.at[g, o + 1], in_s.at[g, o], in_r.at[g, o], right)

    def pass_out(g, o):
        return remote(osend.at[g, o], orecv.at[g, o], out_s.at[g, o], out_r.at[g, o], left)

    def share_x(r):
        return remote(x_ref.at[:, in_slot(r)], xin.at[r], x_s.at[r], x_r.at[r], in_team(r))

    def in_slot(r):
        return lax.rem(core + r // NX, 2) * NX + lax.rem(x + lax.rem(r, NX), NX)

    own_x = pltpu.make_async_copy(x_ref.at[:, in_slot(0)], xin.at[0], x_own)

    def do_in0(g):
        for copy in own_kv(g):
            copy.wait()
        pass_in(g, 0).start()

    def do_in1(g):
        pass_in(g, 0).wait_recv()
        pass_in(g, 1).start()

    def do_in2(g):
        pass_in(g, 1).wait_recv()
        pass_in(g, 2).start()

    def nt(a, b):
        return lax.dot_general(a, b, (((1,), (1,)), ((), ())), preferred_element_type=f32)

    def leave_dq(g, half):
        cols = pl.ds(pl.multiple_of((g * MEMBERS + half * HALF) * DH, HALF * DH), HALF * DH)
        return pltpu.make_async_copy(dq_ref.at[:, cols], dq_hbm.at[:, cols], dq_s.at[g, half])

    def do_att(g, half):
        keys = kv[g, :, 0].reshape(4 * TOK, DH)
        values = kv[g, :, 1].reshape(4 * TOK, DH)
        base = (g * MEMBERS + half * HALF) * DH
        group = pl.ds(pl.multiple_of(base, HALF * DH), HALF * DH)

        def heads_of(ref):
            wide = ref[:, group]
            return [wide[:, j * DH:(j + 1) * DH] for j in range(HALF)]

        queries, grads = heads_of(q_ref), heads_of(og_ref)
        low_probs, dscores = [], []
        for j in range(HALF):
            scores = nt(keys, queries[j]) + bias[...]
            dprobs = nt(values, grads[j])
            top = jnp.max(scores, axis=0, keepdims=True)
            weights = jnp.exp2((scores - top) * (LOG2E * DH ** -0.5))
            p = weights * (1.0 / jnp.sum(weights, axis=0, keepdims=True))
            delta = jnp.sum(p * dprobs, axis=0, keepdims=True)
            low_probs.append(p.astype(bf16))
            dscores.append((p * (dprobs - delta)).astype(bf16))
        ds = jnp.concatenate(dscores, axis=1)
        dk = jnp.dot(ds, jnp.concatenate(queries, axis=0), preferred_element_type=f32)
        dv = jnp.dot(
            jnp.concatenate(low_probs, axis=1), jnp.concatenate(grads, axis=0),
            preferred_element_type=f32,
        )
        new = jnp.concatenate([dk * (DH ** -0.5), dv], axis=1).reshape(SPAN + 1, TOK, 2 * DH)
        dqt = jnp.dot(keys.T, ds, preferred_element_type=f32) * (DH ** -0.5)
        dq_ref[:, group] = jnp.concatenate(
            [dqt[:, j * TOK:(j + 1) * TOK].T for j in range(HALF)], axis=1
        ).astype(bf16)
        leave_dq(g, half).start()

        @pl.when(half == 0)
        def _():
            parts[g] = new

        @pl.when(half == 1)
        def _():
            total = parts[g] + new
            parts[g] = total
            osend[g, 0] = total[SPAN].astype(bf16)
            pass_out(g, 0).start()

    def do_out2(g):
        pass_out(g, 0).wait_recv()
        osend[g, 1] = (orecv[g, 0].astype(f32) + parts[g, 2]).astype(bf16)
        pass_out(g, 1).start()

    def do_out3(g):
        pass_out(g, 1).wait_recv()
        osend[g, 2] = (orecv[g, 1].astype(f32) + parts[g, 1]).astype(bf16)
        pass_out(g, 2).start()

    def share_rows(g, r):
        return remote(rows.at[g, 0], rows.at[g, r], ag_s.at[g], ag_r.at[g, r], in_team(r))

    def share_mate(g):
        return remote(
            rows.at[g, pl.ds(1, NX - 1)], rows.at[g, pl.ds(NX + 1, NX - 1)],
            mate_s.at[g], mate_r.at[g], in_team(NX),
        )

    def do_mate(g):
        def receive(r, carry):
            share_rows(g, r).wait_recv()
            return carry

        lax.fori_loop(1, NX, receive, 0)
        share_mate(g).start()

    def do_out4(g):
        pass_out(g, 2).wait_recv()
        rows[g, 0] = (orecv[g, 2].astype(f32) + parts[g, 0]).astype(bf16)

        def send(r, carry):
            share_rows(g, r).start()
            return carry

        lax.fori_loop(1, NX + 1, send, 0)

    def share_y(g, s):
        return remote(
            ksend.at[g, lax.rem(y + s, NY)], krecv.at[g, s - 1], y_s.at[g], y_r.at[g], in_y(s)
        )

    def share_z(g, s):
        return remote(
            vsend.at[g, lax.rem(z + s, NZ)], vrecv.at[g, s - 1], z_s.at[g], z_r.at[g], in_z(s)
        )

    def last_z(g, s):
        return remote(
            ksum.at[g, lax.rem(z + s, NZ)], klast.at[g, s - 1], z2_s.at[g], z2_r.at[g], in_z(s)
        )

    def last_y(g, s):
        return remote(
            vsum.at[g, lax.rem(y + s, NY)], vlast.at[g, s - 1], y2_s.at[g], y2_r.at[g], in_y(s)
        )

    def do_mul(g):
        share_rows(g, NX).wait_recv()
        share_mate(g).wait_recv()
        taken = jnp.concatenate(
            [xin[r].reshape(NY * 64, TOK) for r in range(8)], axis=1
        )
        out = jnp.dot(taken, rows[g].reshape(8 * TOK, 2 * DH), preferred_element_type=f32)
        ksend[g] = out[:, :DH].astype(bf16).reshape(NY, 64, DH)
        by_z = [out[(i * NZ + k) * 8:(i * NZ + k + 1) * 8, DH:] for k in range(NZ) for i in range(NY)]
        vsend[g] = jnp.concatenate(by_z, axis=0).astype(bf16).reshape(NZ, 64, DH)

        def send(s, carry):
            s = lax.rem(s * 3, NY)
            share_y(g, s).start()
            share_z(g, s).start()
            return carry

        lax.fori_loop(1, NY, send, 0)

    def do_sumy(g):
        arrived(krecv.at[g], y_r.at[g])
        total = ksend[g, y].astype(f32)
        for s in range(NY - 1):
            total = total + krecv[g, s].astype(f32)
        ksum[g] = total.reshape(NZ, 8, DH)
        arrived(vrecv.at[g], z_r.at[g])
        total = vsend[g, z].astype(f32)
        for s in range(NZ - 1):
            total = total + vrecv[g, s].astype(f32)
        vsum[g] = total.reshape(NY, 8, DH)

        def send(s, carry):
            s = lax.rem(s * 3, NZ)
            last_z(g, s).start()
            last_y(g, s).start()
            return carry

        lax.fori_loop(1, NZ, send, 0)

    norm = (NX * NY * NZ * 2 * TOK) ** -0.5

    def do_sumz(g):
        arrived(klast.at[g], z2_r.at[g])
        arrived(vlast.at[g], y2_r.at[g])
        key_total, value_total = ksum[g, z], vsum[g, y]
        for s in range(NZ - 1):
            key_total = key_total + klast[g, s]
            value_total = value_total + vlast[g, s]
        w_ref[:, pl.ds(pl.multiple_of(g * DH, DH), DH)] = key_total * norm
        w_ref[:, pl.ds(pl.multiple_of((HEADS + g) * DH, DH), DH)] = value_total * norm

    def step(t, carry):
        at(t, IN1, do_in1, 1)
        at(t, IN2, do_in2, 1)

        @pl.when(t == SEND_X)
        def _():
            own_x.start()

            def send(r, inner):
                share_x(r).start()
                return inner

            lax.fori_loop(1, 8, send, 0)

        at(t, OUT2, do_out2)
        at(t, OUT3, do_out3)
        at(t, OUT4, do_out4)
        at(t, MATE, do_mate)

        @pl.when(t == MUL)
        def _():
            own_x.wait()

            def receive(r, inner):
                share_x(r).wait_recv()
                return inner

            lax.fori_loop(1, 8, receive, 0)

        at(t, MUL, do_mul)
        at(t, SUMY, do_sumy)
        at(t, SUMZ, do_sumz)

        @pl.when(t == ATT)
        def _():
            loads[1].wait()
            loads[2].wait()

        late = t - ATT

        @pl.when((late >= 0) & (late < 2 * HEADS))
        def _():
            g = jnp.clip(late // 2, 0, HEADS - 1)
            half = lax.rem(late + 2, 2)

            @pl.when(half == 0)
            def _():
                pass_in(g, 2).wait_recv()

            do_att(g, half)

        return carry

    def start_in(g, carry):
        do_in0(g)
        return carry

    lax.fori_loop(0, HEADS, start_in, 0)
    lax.fori_loop(0, STEPS, step, 0)

    def sent_x(r, carry):
        share_x(r).wait_send()
        return carry

    lax.fori_loop(1, 8, sent_x, 0)

    def sent(g, carry):
        for o in range(SPAN):
            pass_in(g, o).wait_send()
            pass_out(g, o).wait_send()
        arrived(rows.at[g, pl.ds(1, NX)], ag_s.at[g])
        share_mate(g).wait_send()
        arrived(krecv.at[g], y_s.at[g])
        arrived(vrecv.at[g], z_s.at[g])
        arrived(klast.at[g], z2_s.at[g])
        arrived(vlast.at[g], y2_s.at[g])
        leave_dq(g, 0).wait()
        leave_dq(g, 1).wait()
        return carry

    lax.fori_loop(0, HEADS, sent, 0)


def shards(query_states, key_states, value_states, out_grad, doc_lengths, layer_inputs):
    rows_dev, width = query_states.shape
    columns = 2 * key_states.shape[1]
    team = 2 * NX
    by_row = layer_inputs.reshape(NY, team, layer_inputs.shape[0] // (NY * team), rows_dev)
    bf16, f32 = jnp.bfloat16, jnp.float32
    vmem = pl.BlockSpec(memory_space=pltpu.VMEM)
    dma = pltpu.SemaphoreType.DMA
    return pl.pallas_call(
        kernel,
        out_shape=(
            jax.ShapeDtypeStruct((rows_dev, width), bf16),
            jax.ShapeDtypeStruct((8, columns), f32),
        ),
        in_specs=[pl.BlockSpec(memory_space=pltpu.HBM)] * 6,
        out_specs=(pl.BlockSpec(memory_space=pltpu.HBM), vmem),
        scratch_shapes=[
            pltpu.SMEM(doc_lengths.shape, jnp.int32),
            pltpu.VMEM((rows_dev, width), bf16),
            pltpu.VMEM((rows_dev, width), bf16),
            pltpu.VMEM((rows_dev, width), bf16),
            pltpu.VMEM((HEADS, SPAN + 1, 2, TOK, DH), bf16),
            pltpu.VMEM((4 * TOK, TOK), f32),
            pltpu.VMEM((HEADS, SPAN + 1, TOK, 2 * DH), f32),
            pltpu.VMEM((HEADS, SPAN, TOK, 2 * DH), bf16),
            pltpu.VMEM((HEADS, SPAN, TOK, 2 * DH), bf16),
            pltpu.VMEM((HEADS, 8, TOK, 2 * DH), bf16),
            pltpu.VMEM((8, NY, 64, TOK), bf16),
            pltpu.VMEM((HEADS, NY, 64, DH), bf16),
            pltpu.VMEM((HEADS, NY - 1, 64, DH), bf16),
            pltpu.VMEM((HEADS, NZ, 64, DH), bf16),
            pltpu.VMEM((HEADS, NZ - 1, 64, DH), bf16),
            pltpu.VMEM((HEADS, NZ, 8, DH), f32),
            pltpu.VMEM((HEADS, NZ - 1, 8, DH), f32),
            pltpu.VMEM((HEADS, NY, 8, DH), f32),
            pltpu.VMEM((HEADS, NY - 1, 8, DH), f32),
            dma((3,)), dma((HEADS, 2)), dma((HEADS, 2)),
            dma((HEADS, SPAN)), dma((HEADS, SPAN)),
            dma((HEADS, SPAN)), dma((HEADS, SPAN)),
            dma((8,)), dma((8,)), dma,
            dma((HEADS,)), dma((HEADS, NX + 1)),
            dma((HEADS,)), dma((HEADS,)),
            dma((HEADS,)), dma((HEADS,)),
            dma((HEADS,)), dma((HEADS,)),
            dma((HEADS,)), dma((HEADS,)), dma((HEADS,)), dma((HEADS,)),
        ],
        compiler_params=pltpu.CompilerParams(
            collective_id=0, has_side_effects=True, vmem_limit_bytes=62 << 20
        ),
        name="attention_and_weight_grad",
    )(doc_lengths, query_states, key_states, value_states, out_grad, by_row)


def solution(mesh):
    whole = P(("dp", "attn"), None)
    return jax.shard_map(
        shards,
        mesh=mesh,
        in_specs=(whole, whole, whole, whole, P("dp", None), P(None, ("dp", "attn"))),
        out_specs=(whole, whole),
        check_vma=False,
    )
```
